512 devices in a mesh: lon: 32 (over x, z_lo, core), ch: 16 (over z_hi, y).
Axes of the slice: x: 4, y: 8, z: 8 (z_hi: 2, z_lo: 4; z = z_hi * 4 + z_lo), core: 2. Of those that a mesh axis runs over, the one named last changes fastest.
Arguments:
- fields: bfloat16 [2, 512, 1440, 128], P(None, 'ch', 'lon'), may hold values from -6 to 6
- zonal_taps: bfloat16 [512, 181], P('ch'), may hold values from -0.4375 to 0.4375
- conv_weight: bfloat16 [512, 16, 3, 3], P('ch'), may hold values from -0.5 to 0.5
- mix_weight: bfloat16 [512, 512], P('ch'), may hold values from -0.25 to 0.25
Outputs:
- updated: bfloat16 [2, 512, 1440, 128], P(None, 'ch', 'lon')
The draws below stay inside these ranges and needn't reach their ends.
All inputs are finite; a program needn't handle non-finite values.
Results may differ from the reference program's by a relative error of at most 0.009.
Values may be sent and summed in bfloat16 or wider, within the bound.
No kernel may reach another device: no remote copies, remote signals or barrier semaphores. Data moves between devices by JAX's collectives and lax.ppermute only.
A program may use at most 64 MiB of HBM per device.

```python
import jax
import jax.numpy as jnp
from jax import lax

CH = 512
GROUPS = 32
GROUP_WIDTH = 16
GROUP_DILATION = 4
MEMBERS = 2
LAT = 128
HALF = 90
LON = 1440


def block_scale(stream_key, shape, pieces, least, top_value):
    loudness = 1.0
    for axis_at, shards_of in pieces:
        heights = jax.random.uniform(jax.random.fold_in(jax.random.fold_in(stream_key, 6), axis_at), (shards_of,), jnp.float32, least / len(pieces), top_value / len(pieces))
        loudness = loudness * jnp.repeat(jnp.exp(heights), shape[axis_at] // shards_of).reshape((-1,) + (1,) * (len(shape) - 1 - axis_at))
    return loudness


def centred(rng, shape, spread, most, split=(), dtype=jnp.bfloat16):
    loudness = block_scale(rng, shape, split, -0.22, 0.18) if split else 1.0
    values = jax.random.normal(rng, shape, jnp.float32) * spread * loudness
    return jnp.minimum(jnp.maximum(values, -most), most).astype(dtype)


def setup_inputs(seed: int = 0) -> dict:
    streams_of = jax.random.split(jax.random.key(seed), 5)
    fields = centred(streams_of[0], (MEMBERS, CH, LON, LAT), 1.0, 6.0, ((1, 16), (2, 32)))
    zonal_taps = centred(streams_of[1], (CH, 2 * HALF + 1), (2 * HALF + 1) ** -0.5, 0.4375, ((0, 16),))
    conv_weight = centred(streams_of[2], (CH, GROUP_WIDTH, 3, 3), (9 * GROUP_WIDTH) ** -0.5, 0.5, ((0, 16),))
    mix_weight = centred(streams_of[3], (CH, CH), CH ** -0.5, 0.25, ((0, 16),))
    return {"fields": fields, "zonal_taps": zonal_taps, "conv_weight": conv_weight, "mix_weight": mix_weight}


def zonal_pass(fields, zonal_taps):
    taps = zonal_taps.astype(jnp.float32)
    offsets = (jnp.arange(2 * HALF + 1) - HALF) % LON
    kernel = jnp.zeros((CH, LON), jnp.float32).at[:, offsets].set(taps)
    kernel_hat = jnp.conj(jnp.fft.rfft(kernel, axis=-1))

    def member(field_one):
        spectrum = jnp.fft.rfft(field_one.astype(jnp.float32), axis=-1)
        result = jnp.fft.irfft(spectrum * kernel_hat[:, None, :], n=LON, axis=-1)
        return result.astype(jnp.float32).astype(jnp.bfloat16)

    return lax.map(member, fields)


def reference(fields, zonal_taps, conv_weight, mix_weight):
    lat_major = jnp.swapaxes(fields, 2, 3)
    zonal_output = zonal_pass(lat_major, zonal_taps)
    periodic_field = jnp.concatenate([zonal_output[..., -GROUP_DILATION:], zonal_output, zonal_output[..., :GROUP_DILATION]], axis=3)
    padded_field = jnp.pad(periodic_field, ((0, 0), (0, 0), (GROUP_DILATION, GROUP_DILATION), (0, 0)))
    mix_full = mix_weight.astype(jnp.float32)
    kernel = conv_weight.astype(jnp.float32)

    def member(padded_one):
        conv = lax.conv_general_dilated(padded_one[None].astype(jnp.float32), kernel, (1, 1), "VALID",
                                        rhs_dilation=(GROUP_DILATION, GROUP_DILATION), dimension_numbers=("NCHW", "OIHW", "NCHW"),
                                        feature_group_count=GROUPS, precision=lax.Precision.HIGHEST)[0]
        hidden = jax.nn.gelu(conv, approximate=False).astype(jnp.bfloat16)
        mixed = jnp.einsum("oi,irl->orl", mix_full, hidden.astype(jnp.float32),
                           precision=lax.Precision.HIGHEST).astype(jnp.bfloat16)
        return mixed

    mixed = jnp.swapaxes(lax.map(member, padded_field), 2, 3)
    return (fields.astype(jnp.float32) + mixed.astype(jnp.float32)).astype(jnp.bfloat16)
```

```python
import jax
import jax.numpy as jnp
from jax import lax
from jax.sharding import PartitionSpec as P

GROUP_WIDTH = 16
GROUP_DILATION = 4


def passed_along(block, axis, distance):
    devices = range(lax.axis_size(axis))
    route = [((i - distance) % len(devices), i) for i in devices]
    return lax.ppermute(block, axis, route)


def extended(block, sides, width):
    for axis, dim in sides:
        count = lax.axis_size(axis)
        forward = [(i, i + 1) for i in range(count - 1)]
        forward.append((count - 1, 0))
        backward = [(target, source) for source, target in forward]
        low = lax.ppermute(
            lax.slice_in_dim(block, block.shape[dim] - width, None, axis=dim), axis, forward
        )
        high = lax.ppermute(lax.slice_in_dim(block, 0, width, axis=dim), axis, backward)
        block = jnp.concatenate([low, block, high], axis=dim)
    return block


def per_device(fields, zonal_taps, conv_weight, mix_weight):
    ensemble_members, chans, field_width, row_block = fields.shape
    sides = {}
    for offset in (1, 2, -1, -2):
        sides[offset] = passed_along(fields, "lon", offset)
    window = jnp.concatenate([sides[2], sides[1], fields, sides[-1], sides[-2]], axis=2)
    offsets = jnp.arange(5 * field_width)[:, None] - jnp.arange(field_width)[None, :]
    inside = (offsets >= 0) & (offsets <= 4 * field_width)
    clipped = jnp.clip(offsets, 0, 4 * field_width)
    toeplitz = jnp.where(inside[None], zonal_taps[:, clipped], jnp.zeros((), jnp.bfloat16))
    zonal_output = jnp.einsum(
        "mcjr,cjl->mclr", window, toeplitz, preferred_element_type=jnp.float32
    ).astype(jnp.bfloat16)
    halo_padded = extended(zonal_output, (("lon", 2),), GROUP_DILATION)
    padded_field = jnp.pad(halo_padded, ((0, 0), (0, 0), (0, 0), (GROUP_DILATION, GROUP_DILATION)))
    local_groups = chans // GROUP_WIDTH
    grouped_output = padded_field.reshape(
        ensemble_members,
        local_groups,
        GROUP_WIDTH,
        field_width + 2 * GROUP_DILATION,
        row_block + 2 * GROUP_DILATION,
    )
    kernel = conv_weight.reshape(local_groups, GROUP_WIDTH, GROUP_WIDTH, 3, 3)
    summed = jnp.zeros(
        (ensemble_members, local_groups, GROUP_WIDTH, field_width, row_block), jnp.float32
    )
    for latitude_taps in range(3):
        for longitude_taps in range(3):
            section = grouped_output[
                :,
                :,
                :,
                longitude_taps * GROUP_DILATION : longitude_taps * GROUP_DILATION + field_width,
                latitude_taps * GROUP_DILATION : latitude_taps * GROUP_DILATION + row_block,
            ]
            summed = summed + jnp.einsum(
                "goi,mgilr->mgolr",
                kernel[:, :, :, latitude_taps, longitude_taps],
                section,
                preferred_element_type=jnp.float32,
            )
    hidden = jax.nn.gelu(
        summed.reshape(ensemble_members, chans, field_width, row_block), approximate=False
    ).astype(jnp.bfloat16)
    count = lax.axis_size("ch")
    rows = ensemble_members * field_width
    share = -(-rows // count)
    by_row = hidden.transpose(0, 2, 1, 3).reshape(rows, chans, row_block)
    by_row = jnp.pad(by_row, ((0, count * share - rows), (0, 0), (0, 0)))
    gathered = lax.all_to_all(
        by_row.reshape(count, share, chans, row_block), "ch", 0, 0, tiled=True
    )
    mix_full = lax.all_gather(mix_weight, "ch", axis=0, tiled=True)
    mixed_rows = jnp.einsum(
        "doci,csir->dsor",
        mix_full.reshape(count, chans, count, chans),
        gathered,
        preferred_element_type=jnp.float32,
    ).astype(jnp.bfloat16)
    returned = lax.all_to_all(mixed_rows, "ch", 0, 0, tiled=True)
    returned = returned.reshape(count * share, chans, row_block)[:rows]
    mixed = returned.reshape(ensemble_members, field_width, chans, row_block).transpose(0, 2, 1, 3)
    return (fields.astype(jnp.float32) + mixed.astype(jnp.float32)).astype(jnp.bfloat16)


def solution(mesh):
    return jax.shard_map(
        per_device,
        mesh=mesh,
        in_specs=(
            P(None, "ch", "lon", None),
            P("ch", None),
            P("ch", None, None, None),
            P("ch", None),
        ),
        out_specs=P(None, "ch", "lon", None),
        check_vma=False,
    )
```

```python
import jax
import jax.numpy as jnp
from jax import lax
from jax.experimental import pallas as pl
from jax.experimental.pallas import tpu as pltpu
from jax.sharding import Mesh, PartitionSpec as P

F32, BF16 = jnp.float32, jnp.bfloat16
MEMBERS, CHANS, WIDTH, LAT = 2, 32, 45, 128
SLOT = 48
GROUP = 16
TALL = 56
BLOCKS = 8
VMEM = pltpu.CompilerParams(vmem_limit_bytes=40 * 1024 * 1024)
CHIPS = (("x", 4), ("zl", 4), ("core", 2), ("zh", 2), ("y", 8))


def lat_shuffle(back):
    rows = lax.broadcasted_iota(jnp.int32, (256, 256), 1 if back else 0)
    cols = lax.broadcasted_iota(jnp.int32, (256, 256), 0 if back else 1)
    chan, lane = (cols % 128) // 64, cols % 64
    source = chan * 128 + 4 * (lane // 2) + 2 * (cols // 128) + lane % 2
    return jnp.where(rows == source, 1.0, 0.0).astype(BF16)


def split_kernel(fields_ref, out_ref, wide):
    shuffle = lat_shuffle(False)
    wide[...] = fields_ref[...].astype(F32).reshape(MEMBERS, WIDTH * CHANS, 128)
    for m in range(MEMBERS):
        for g in range(2):
            for c in range(8):
                sides = [
                    wide[m, pl.ds(g * GROUP + part * 8 + c, WIDTH, stride=CHANS), :].astype(BF16)
                    for part in range(2)
                ]
                both = jnp.concatenate(sides, axis=1)
                moved = jnp.dot(both, shuffle, preferred_element_type=F32).astype(BF16)
                for s in range(2):
                    out_ref[m, s, g, c, 32:48] = jnp.zeros((16, 128), BF16)
                    out_ref[m, s, g, c, 0:WIDTH] = moved[:, s * 128 : s * 128 + 128]


def toeplitz_kernel(taps_ref, out_ref):
    lane = lax.broadcasted_iota(jnp.int32, (TALL, 256), 1)
    for c in range(GROUP):
        row = jnp.broadcast_to(taps_ref[c : c + 1, :], (TALL, 256))
        base = pltpu.roll(row, 0, 1, stride=1, stride_axis=0)
        full = pltpu.roll(base, 252, 1)
        for k in range(1, 5):
            full = jnp.where(lane >= SLOT * k, pltpu.roll(base, (3 * k - 4) % 256, 1), full)
        full = jnp.where(lane >= 240, pltpu.roll(base, 11, 1), full)
        full = jnp.where(lane >= 248, pltpu.roll(base, 249, 1), full)
        out_ref[c] = full.astype(BF16)


def turned(v):
    return jnp.concatenate([v[:, 64:], v[:, :64]], axis=1)


def rim_kernel(run_ref, unused_ref, low_ref, high_ref):
    low_ref[:, 0:16] = run_ref[5, :, 32:48]
    low_ref[:, 16:64] = run_ref[6]
    low_ref[:, 64:112] = run_ref[7]
    high_ref[:, 0:48] = run_ref[0]
    high_ref[:, 48:96] = run_ref[1]
    high_ref[:, 96:112] = run_ref[2, :, 0:16]


def conv_kernel(unused_ref, low_ref, mid_ref, high_ref, toep_ref, weight_ref, out_ref, zonal, shifted):
    lane = lax.broadcasted_iota(jnp.int32, (SLOT, 128), 1)
    first_half = lane < 64
    tile_row = lax.broadcasted_iota(jnp.int32, (16, 128), 0)

    def block(b, c):
        if 0 <= b < BLOCKS:
            return mid_ref[b, c]
        if b < 0:
            return low_ref[c, 16 + SLOT * (b + 2) : 16 + SLOT * (b + 3)]
        return high_ref[c, SLOT * (b - BLOCKS) : SLOT * (b - BLOCKS + 1)]

    def one_pair(c):
        blocks = {b: block(b, c) for b in range(-2, BLOCKS + 2)}
        tails = {b: blocks[b][32:48] if b >= -2 else low_ref[c, 0:16] for b in range(-3, 5)}
        heads = {
            b: blocks[b][0:16] if b < BLOCKS + 2 else high_ref[c, 2 * SLOT : 2 * SLOT + 16]
            for b in range(3, BLOCKS + 3)
        }
        blocks_turned = {b: turned(v) for b, v in blocks.items()}
        tails_turned = {b: turned(v) for b, v in tails.items()}
        heads_turned = {b: turned(v) for b, v in heads.items()}
        for part in range(2):

            def paired(plain, other, b):
                low, high = (plain, other) if part == 0 else (other, plain)
                return jnp.where(first_half[: low[b].shape[0]], low[b], high[b + 4])

            wide = {b: paired(blocks, blocks_turned, b) for b in range(-2, 6)}
            taps = toep_ref[part * 8 + c]
            for b in range(4):
                rim = jnp.where(
                    tile_row >= 8,
                    paired(tails, tails_turned, b - 3),
                    paired(heads, heads_turned, b + 3),
                )
                window = jnp.concatenate([wide[b + k] for k in range(-2, 3)] + [rim], axis=0)
                result = jnp.dot(taps, window, preferred_element_type=F32)
                zonal[pl.ds(b * TALL * GROUP + part * 8 + c, TALL, stride=GROUP), :] = result

    for c in range(8):
        one_pair(c)

    place = lax.broadcasted_iota(jnp.int32, (TALL * GROUP, 128), 1) % 64
    for b in range(4):
        z = zonal[b * TALL * GROUP : (b + 1) * TALL * GROUP, :]
        south = jnp.where(place < 2, 0.0, pltpu.roll(z, 2, 1))
        north = jnp.where(place >= 62, 0.0, pltpu.roll(z, 126, 1))
        for a, v in enumerate((south, z, north)):
            shifted[b, a] = v.astype(BF16).reshape(TALL, GROUP, 128)

    weight = weight_ref[...]

    def three_columns(n, carry):
        for half in range(2):
            for i in range(3):
                col = n * 3 + i
                sides = []
                for top in range(2):
                    tiles = [
                        shifted[half + 2 * top, a, col + 4 * b] for b in range(3) for a in range(3)
                    ]
                    sides.append(jnp.concatenate(tiles, axis=0))
                x = jnp.dot(weight, jnp.concatenate(sides, axis=1), preferred_element_type=F32)
                x = 0.5 * x * (1.0 + lax.erf(x * 0.7071067811865476))
                x = x.astype(BF16)
                for top in range(2):
                    out_ref[half * 16 + n, top * 3 + i] = x[:, top * 128 : top * 128 + 128]
        return carry

    lax.fori_loop(0, 15, three_columns, 0)
    for half in range(2):
        for i in range(6):
            out_ref[half * 16 + 15, i] = jnp.zeros((GROUP, 128), BF16)


def mix_kernel(owner_ref, weight_ref, hidden_ref, out_ref):
    first_half = lax.broadcasted_iota(jnp.int32, (GROUP, 128), 1) < 64
    weight = weight_ref[...].reshape(512, 512)
    for i in range(3):
        cols = [hidden_ref[:, top * 3 + i].reshape(512, 128) for top in range(2)]
        y = jnp.dot(weight, jnp.concatenate(cols, axis=1), preferred_element_type=F32)
        y = y.astype(BF16)
        for ch in range(16):
            owner = owner_ref[ch]
            for top in range(2):
                a = y[ch * 32 : ch * 32 + 16, top * 128 : top * 128 + 128]
                b = y[ch * 32 + 16 : ch * 32 + 32, top * 128 : top * 128 + 128]
                out_ref[top, owner, i] = jnp.where(first_half, a, turned(b))
                out_ref[2 + top, owner, i] = jnp.where(first_half, turned(a), b)


def join_kernel(mixed_ref, fields_ref, out_ref):
    shuffle = lat_shuffle(True)
    for m in range(MEMBERS):
        both = jnp.concatenate(
            [mixed_ref[m, s, 0:WIDTH].reshape(WIDTH * GROUP, 128) for s in range(2)], axis=1
        )
        y = jnp.dot(both, shuffle, preferred_element_type=F32).reshape(WIDTH, GROUP, 256)
        for part in range(2):
            rows = slice(part * GROUP, part * GROUP + GROUP)
            total = fields_ref[m, :, rows].astype(F32) + y[:, :, part * 128 : part * 128 + 128]
            out_ref[m, :, rows] = total.astype(BF16)


def kernel_call(body, shape, scratch=(), cost=(0, 0), **specs):
    return pl.pallas_call(
        body,
        **specs,
        out_shape=shape if isinstance(shape, list) else jax.ShapeDtypeStruct(shape, BF16),
        scratch_shapes=list(scratch),
        compiler_params=VMEM,
        cost_estimate=pl.CostEstimate(flops=cost[0], bytes_accessed=cost[1], transcendentals=0),
    )


def with_behind(blocks, axis, *steps):
    count = lax.axis_size(axis)
    parts = [blocks]
    for step in steps:
        parts.append(lax.ppermute(blocks, axis, [(i, (i + step) % count) for i in range(count)]))
    return jnp.concatenate(parts, axis=0)


def block_owners():
    i = jnp.arange(16)
    zh = (lax.axis_index("zh") + i // 8) % 2
    y = (lax.axis_index("y") - 2 * (i % 4) - i // 4 % 2) % 8
    return (zh * 8 + y).astype(jnp.int32)


def per_device(fields, zonal_taps, conv_weight, mix_weight):
    core = lax.axis_index("core")
    vmem = pl.BlockSpec(memory_space=pltpu.VMEM)
    loose = pl.BlockSpec(memory_space=pl.ANY)
    by_group = mix_weight.reshape(CHANS, 16, 2, GROUP).transpose(0, 2, 1, 3).reshape(CHANS, 512)
    few = with_behind(with_behind(by_group[None], "y", 2, 4, 6), "y", 1)
    mix_full = with_behind(few, "zh", 1)

    columns = fields.transpose(0, 2, 1, 3)
    units = kernel_call(
        split_kernel,
        (2, 2, 2, 8, SLOT, 128),
        scratch=(pltpu.VMEM((MEMBERS, WIDTH * CHANS, 128), F32),),
        cost=(2 * 10**8, 3 * 10**6),
    )(columns)
    run = lax.all_to_all(
        units.reshape(BLOCKS, 8, SLOT, 128), ("zl", "core"), 0, 0, tiled=True
    )
    taps = lax.dynamic_slice_in_dim(zonal_taps, core * GROUP, GROUP, 0).astype(F32)
    taps = jnp.pad(taps, ((0, 0), (0, 256 - taps.shape[1])))
    toeplitz = kernel_call(toeplitz_kernel, (GROUP, TALL, 256), cost=(10**7, 10**6))(taps)
    weight = lax.dynamic_slice_in_dim(conv_weight, core * GROUP, GROUP, 0)
    weight = weight.transpose(0, 3, 2, 1).reshape(GROUP, 9 * GROUP)

    count = lax.axis_size("x")
    east = [(i, (i + 1) % count) for i in range(count)]
    west = [(b, a) for a, b in east]
    rim = jax.ShapeDtypeStruct((8, 112, 128), BF16)
    low, high = kernel_call(rim_kernel, [rim, rim], in_specs=[vmem, loose], cost=(0, 10**6))(run, few)
    low = lax.ppermute(low, "x", east)
    high = lax.ppermute(high, "x", west)

    hidden = kernel_call(
        conv_kernel,
        (32, 6, GROUP, 128),
        scratch=(
            pltpu.VMEM((4 * TALL * GROUP, 128), F32),
            pltpu.VMEM((4, 3, TALL, GROUP, 128), BF16),
        ),
        cost=(10**9, 3 * 10**6),
        in_specs=[loose] + [vmem] * 5,
    )(mix_full, low, run, high, toeplitz, weight)
    gathered = lax.all_to_all(hidden, ("core", "zh", "y"), 0, 0, tiled=True)
    mixed = kernel_call(
        mix_kernel,
        (4, 16, 3, GROUP, 128),
        cost=(4 * 10**8, 2 * 10**6),
        in_specs=[pl.BlockSpec(memory_space=pltpu.SMEM), vmem, vmem],
    )(block_owners(), mix_full, gathered)
    back = lax.all_to_all(mixed.reshape(64, 3, GROUP, 128), ("zl", "zh", "y"), 0, 0, tiled=True)
    updated = kernel_call(join_kernel, columns.shape, cost=(2 * 10**8, 3 * 10**6))(
        back.reshape(MEMBERS, 2, SLOT, GROUP, 128), columns
    )
    return updated.transpose(0, 2, 1, 3)


def solution(mesh):
    names, sizes = zip(*CHIPS)
    chips = Mesh(mesh.devices.reshape(sizes), names)
    lon, ch = ("x", "zl", "core"), ("zh", "y")
    return jax.shard_map(
        per_device,
        mesh=chips,
        in_specs=(P(None, ch, lon, None), P(ch, None), P(ch, None, None, None), P(ch, None)),
        out_specs=P(None, ch, lon, None),
        check_vma=False,
    )
```

```python
import jax
import jax.numpy as jnp
from jax import lax
from jax.experimental import pallas as pl
from jax.experimental.pallas import tpu as pltpu
from jax.sharding import Mesh, PartitionSpec as P

F32, BF16 = jnp.float32, jnp.bfloat16
MEMBERS, CHANS, WIDTH, LAT = 2, 32, 45, 128
SLOT = 48
GROUP = 16
TALL = 56
BLOCKS = 8
VMEM = pltpu.CompilerParams(vmem_limit_bytes=40 * 1024 * 1024)
CHIPS = (("x", 4), ("zl", 4), ("core", 2), ("zh", 2), ("y", 8))


def lat_shuffle(back):
    rows = lax.broadcasted_iota(jnp.int32, (256, 256), 1 if back else 0)
    cols = lax.broadcasted_iota(jnp.int32, (256, 256), 0 if back else 1)
    chan, lane = (cols % 128) // 64, cols % 64
    source = chan * 128 + 4 * (lane // 2) + 2 * (cols // 128) + lane % 2
    return jnp.where(rows == source, 1.0, 0.0).astype(BF16)


def split_kernel(fields_ref, out_ref, wide):
    shuffle = lat_shuffle(False)
    wide[...] = fields_ref[...].astype(F32).reshape(MEMBERS, WIDTH * CHANS, 128)
    for m in range(MEMBERS):
        for g in range(2):
            for c in range(8):
                sides = [
                    wide[m, pl.ds(g * GROUP + part * 8 + c, WIDTH, stride=CHANS), :].astype(BF16)
                    for part in range(2)
                ]
                both = jnp.concatenate(sides, axis=1)
                moved = jnp.dot(both, shuffle, preferred_element_type=F32).astype(BF16)
                for s in range(2):
                    out_ref[m, s, g, c, 32:48] = jnp.zeros((16, 128), BF16)
                    out_ref[m, s, g, c, 0:WIDTH] = moved[:, s * 128 : s * 128 + 128]


def toeplitz_kernel(taps_ref, out_ref):
    lane = lax.broadcasted_iota(jnp.int32, (TALL, 256), 1)
    for c in range(GROUP):
        row = jnp.broadcast_to(taps_ref[c : c + 1, :], (TALL, 256))
        base = pltpu.roll(row, 0, 1, stride=1, stride_axis=0)
        full = pltpu.roll(base, 252, 1)
        for k in range(1, 5):
            full = jnp.where(lane >= SLOT * k, pltpu.roll(base, (3 * k - 4) % 256, 1), full)
        full = jnp.where(lane >= 240, pltpu.roll(base, 11, 1), full)
        full = jnp.where(lane >= 248, pltpu.roll(base, 249, 1), full)
        out_ref[c] = full.astype(BF16)


def turned(v):
    return jnp.concatenate([v[:, 64:], v[:, :64]], axis=1)


def rim_kernel(run_ref, low_ref, high_ref):
    low_ref[:, 0:16] = run_ref[5, :, 32:48]
    low_ref[:, 16:64] = run_ref[6]
    low_ref[:, 64:112] = run_ref[7]
    high_ref[:, 0:48] = run_ref[0]
    high_ref[:, 48:96] = run_ref[1]
    high_ref[:, 96:112] = run_ref[2, :, 0:16]


def zonal_kernel(low_ref, mid_ref, high_ref, toep_ref, zonal):
    lane = lax.broadcasted_iota(jnp.int32, (SLOT, 128), 1)
    first_half = lane < 64
    tile_row = lax.broadcasted_iota(jnp.int32, (16, 128), 0)

    def block(b, c):
        if 0 <= b < BLOCKS:
            return mid_ref[b, c]
        if b < 0:
            return low_ref[c, 16 + SLOT * (b + 2) : 16 + SLOT * (b + 3)]
        return high_ref[c, SLOT * (b - BLOCKS) : SLOT * (b - BLOCKS + 1)]

    def one_pair(c):
        blocks = {b: block(b, c) for b in range(-2, BLOCKS + 2)}
        tails = {b: blocks[b][32:48] if b >= -2 else low_ref[c, 0:16] for b in range(-3, 5)}
        heads = {
            b: blocks[b][0:16] if b < BLOCKS + 2 else high_ref[c, 2 * SLOT : 2 * SLOT + 16]
            for b in range(3, BLOCKS + 3)
        }
        blocks_turned = {b: turned(v) for b, v in blocks.items()}
        tails_turned = {b: turned(v) for b, v in tails.items()}
        heads_turned = {b: turned(v) for b, v in heads.items()}
        for part in range(2):

            def paired(plain, other, b):
                low, high = (plain, other) if part == 0 else (other, plain)
                return jnp.where(first_half[: low[b].shape[0]], low[b], high[b + 4])

            wide = {b: paired(blocks, blocks_turned, b) for b in range(-2, 6)}
            taps = toep_ref[part * 8 + c]
            windows = []
            for b in range(4):
                rim = jnp.where(
                    tile_row >= 8,
                    paired(tails, tails_turned, b - 3),
                    paired(heads, heads_turned, b + 3),
                )
                windows.append(
                    jnp.concatenate([wide[b + k] for k in range(-2, 3)] + [rim], axis=0)
                )
            for b in (0, 2):
                window = jnp.concatenate(windows[b : b + 2], axis=1)
                result = jnp.dot(taps, window, preferred_element_type=F32)
                for k in range(2):
                    first = (b + k) * TALL * GROUP + part * 8 + c
                    zonal[pl.ds(first, TALL, stride=GROUP), :] = result[:, k * 128 : k * 128 + 128]

    for c in range(8):
        one_pair(c)


def conv_kernel(unused_ref, zonal, weight_ref, out_ref, shifted):
    place = lax.broadcasted_iota(jnp.int32, (TALL * GROUP, 128), 1) % 64
    for b in range(4):
        z = zonal[b * TALL * GROUP : (b + 1) * TALL * GROUP, :].astype(BF16)
        zero = jnp.zeros_like(z)
        south = jnp.where(place < 2, zero, jnp.concatenate([z[:, 126:], z[:, :126]], axis=1))
        north = jnp.where(place >= 62, zero, jnp.concatenate([z[:, 2:], z[:, :2]], axis=1))
        for a, v in enumerate((south, z, north)):
            shifted[b, a] = v.reshape(TALL, GROUP, 128)

    weight = weight_ref[...]

    def three_columns(n, carry):
        for half in range(2):
            for i in range(3):
                col = n * 3 + i
                sides = []
                for top in range(2):
                    tiles = [
                        shifted[half + 2 * top, a, col + 4 * b] for b in range(3) for a in range(3)
                    ]
                    sides.append(jnp.concatenate(tiles, axis=0))
                x = jnp.dot(weight, jnp.concatenate(sides, axis=1), preferred_element_type=F32)
                x = 0.5 * x * (1.0 + lax.erf(x * 0.7071067811865476))
                x = x.astype(BF16)
                for top in range(2):
                    out_ref[half * 16 + n, top * 3 + i] = x[:, top * 128 : top * 128 + 128]
        return carry

    lax.fori_loop(0, 15, three_columns, 0)
    for half in range(2):
        for i in range(6):
            out_ref[half * 16 + 15, i] = jnp.zeros((GROUP, 128), BF16)


def mix_kernel(owner_ref, weight_ref, hidden_ref, out_ref):
    first_half = lax.broadcasted_iota(jnp.int32, (GROUP, 128), 1) < 64
    weight = weight_ref[...].reshape(512, 512)
    for i in range(3):
        cols = [hidden_ref[:, top * 3 + i].reshape(512, 128) for top in range(2)]
        y = jnp.dot(weight, jnp.concatenate(cols, axis=1), preferred_element_type=F32)
        y = y.astype(BF16)
        for ch in range(16):
            owner = owner_ref[ch]
            for top in range(2):
                a = y[ch * 32 : ch * 32 + 16, top * 128 : top * 128 + 128]
                b = y[ch * 32 + 16 : ch * 32 + 32, top * 128 : top * 128 + 128]
                out_ref[top, owner, i] = jnp.where(first_half, a, turned(b))
                out_ref[2 + top, owner, i] = jnp.where(first_half, turned(a), b)


def join_kernel(mixed_ref, fields_ref, out_ref):
    shuffle = lat_shuffle(True)
    for m in range(MEMBERS):
        both = jnp.concatenate(
            [mixed_ref[m, s, 0:WIDTH].reshape(WIDTH * GROUP, 128) for s in range(2)], axis=1
        )
        y = jnp.dot(both, shuffle, preferred_element_type=F32).reshape(WIDTH, GROUP, 256)
        for part in range(2):
            rows = slice(part * GROUP, part * GROUP + GROUP)
            total = fields_ref[m, :, rows].astype(F32) + y[:, :, part * 128 : part * 128 + 128]
            out_ref[m, :, rows] = total.astype(BF16)


def kernel_call(body, shape, scratch=(), cost=(0, 0), **specs):
    return pl.pallas_call(
        body,
        **specs,
        out_shape=shape if isinstance(shape, list) else jax.ShapeDtypeStruct(shape, BF16),
        scratch_shapes=list(scratch),
        compiler_params=VMEM,
        cost_estimate=pl.CostEstimate(flops=cost[0], bytes_accessed=cost[1], transcendentals=0),
    )


def from_behind(blocks, axis, step):
    count = lax.axis_size(axis)
    return lax.ppermute(blocks, axis, [(i, (i + step) % count) for i in range(count)])


def block_owners():
    i = jnp.arange(16)
    i = jnp.where(i < 8, i, 8 + (i + 4 * lax.axis_index("core")) % 8)
    zh = (lax.axis_index("zh") + i // 8) % 2
    y = (lax.axis_index("y") - 4 + i) % 8
    return (zh * 8 + y).astype(jnp.int32)


def per_device(fields, zonal_taps, conv_weight, mix_weight):
    core = lax.axis_index("core")
    vmem = pl.BlockSpec(memory_space=pltpu.VMEM)
    loose = pl.BlockSpec(memory_space=pl.ANY)
    by_group = mix_weight.reshape(CHANS, 16, 2, GROUP).transpose(0, 2, 1, 3).reshape(CHANS, 512)
    few = by_group[None]
    few = jnp.concatenate([from_behind(few, "y", 1), few, from_behind(few, "y", -1)], axis=0)
    few = jnp.concatenate(
        [from_behind(few, "y", 3), few, from_behind(few[:2], "y", -3)], axis=0
    )
    half = from_behind(lax.dynamic_slice_in_dim(few, 4 * core, 4, 0), "zh", 1)
    mix_full = jnp.concatenate([few, half, from_behind(half, "core", 1)], axis=0)

    columns = fields.transpose(0, 2, 1, 3)
    units = kernel_call(
        split_kernel,
        (2, 2, 2, 8, SLOT, 128),
        scratch=(pltpu.VMEM((MEMBERS, WIDTH * CHANS, 128), F32),),
        cost=(2 * 10**8, 3 * 10**6),
    )(columns)
    run = lax.all_to_all(
        units.reshape(BLOCKS, 8, SLOT, 128), ("zl", "core"), 0, 0, tiled=True
    )
    taps = lax.dynamic_slice_in_dim(zonal_taps, core * GROUP, GROUP, 0).astype(F32)
    taps = jnp.pad(taps, ((0, 0), (0, 256 - taps.shape[1])))
    toeplitz = kernel_call(toeplitz_kernel, (GROUP, TALL, 256), cost=(10**7, 10**6))(taps)
    weight = lax.dynamic_slice_in_dim(conv_weight, core * GROUP, GROUP, 0)
    weight = weight.transpose(0, 3, 2, 1).reshape(GROUP, 9 * GROUP)

    count = lax.axis_size("x")
    east = [(i, (i + 1) % count) for i in range(count)]
    west = [(b, a) for a, b in east]
    rim = jax.ShapeDtypeStruct((8, 112, 128), BF16)
    low, high = kernel_call(rim_kernel, [rim, rim], cost=(0, 10**6))(run)
    low = lax.ppermute(low, "x", east)
    high = lax.ppermute(high, "x", west)

    zonal_shape = [jax.ShapeDtypeStruct((4 * TALL * GROUP, 128), F32)]
    zonal = kernel_call(zonal_kernel, zonal_shape, cost=(10**9, 3 * 10**6))(
        low, run, high, toeplitz
    )[0]
    hidden = kernel_call(
        conv_kernel,
        (32, 6, GROUP, 128),
        scratch=(pltpu.VMEM((4, 3, TALL, GROUP, 128), BF16),),
        cost=(10**9, 3 * 10**6),
        in_specs=[loose, vmem, vmem],
    )(half, zonal, weight)
    gathered = lax.all_to_all(hidden, ("core", "zh", "y"), 0, 0, tiled=True)
    mixed = kernel_call(
        mix_kernel,
        (4, 16, 3, GROUP, 128),
        cost=(4 * 10**8, 2 * 10**6),
        in_specs=[pl.BlockSpec(memory_space=pltpu.SMEM), vmem, vmem],
    )(block_owners(), mix_full, gathered)
    back = lax.all_to_all(mixed.reshape(64, 3, GROUP, 128), ("zl", "zh", "y"), 0, 0, tiled=True)
    updated = kernel_call(join_kernel, columns.shape, cost=(2 * 10**8, 3 * 10**6))(
        back.reshape(MEMBERS, 2, SLOT, GROUP, 128), columns
    )
    return updated.transpose(0, 2, 1, 3)


def solution(mesh):
    names, sizes = zip(*CHIPS)
    chips = Mesh(mesh.devices.reshape(sizes), names)
    lon, ch = ("x", "zl", "core"), ("zh", "y")
    return jax.shard_map(
        per_device,
        mesh=chips,
        in_specs=(P(None, ch, lon, None), P(ch, None), P(ch, None, None, None), P(ch, None)),
        out_specs=P(None, ch, lon, None),
        check_vma=False,
    )
```

```python
import jax
import jax.numpy as jnp
from jax import lax
from jax.experimental import pallas as pl
from jax.experimental.pallas import tpu as pltpu
from jax.sharding import Mesh, PartitionSpec as P

F32, BF16 = jnp.float32, jnp.bfloat16
MEMBERS, CHANS, WIDTH, LAT = 2, 32, 45, 128
SLOT = 48
GROUP = 16
TALL = 56
BLOCKS = 8
VMEM = pltpu.CompilerParams(vmem_limit_bytes=40 * 1024 * 1024)
CHIPS = (("x", 4), ("zl", 4), ("core", 2), ("zh", 2), ("y", 8))


def lat_shuffle(back):
    rows = lax.broadcasted_iota(jnp.int32, (256, 256), 1 if back else 0)
    cols = lax.broadcasted_iota(jnp.int32, (256, 256), 0 if back else 1)
    chan, lane = (cols % 128) // 64, cols % 64
    source = chan * 128 + 4 * (lane // 2) + 2 * (cols // 128) + lane % 2
    return jnp.where(rows == source, 1.0, 0.0).astype(BF16)


def split_kernel(fields_ref, out_ref, wide):
    shuffle = lat_shuffle(False)
    wide[...] = fields_ref[0].astype(F32).reshape(WIDTH * CHANS, 128)
    for g in range(2):
        for c in range(8):
            sides = [
                wide[pl.ds(g * GROUP + part * 8 + c, WIDTH, stride=CHANS), :].astype(BF16)
                for part in range(2)
            ]
            both = jnp.concatenate(sides, axis=1)
            moved = jnp.dot(both, shuffle, preferred_element_type=F32).astype(BF16)
            for s in range(2):
                out_ref[0, s, g, c, 32:48] = jnp.zeros((16, 128), BF16)
                out_ref[0, s, g, c, 0:WIDTH] = moved[:, s * 128 : s * 128 + 128]


def toeplitz_kernel(taps_ref, out_ref):
    lane = lax.broadcasted_iota(jnp.int32, (TALL, 256), 1)
    for c in range(GROUP):
        row = jnp.broadcast_to(taps_ref[c : c + 1, :], (TALL, 256))
        base = pltpu.roll(row, 0, 1, stride=1, stride_axis=0)
        full = pltpu.roll(base, 252, 1)
        for k in range(1, 5):
            full = jnp.where(lane >= SLOT * k, pltpu.roll(base, (3 * k - 4) % 256, 1), full)
        full = jnp.where(lane >= 240, pltpu.roll(base, 11, 1), full)
        full = jnp.where(lane >= 248, pltpu.roll(base, 249, 1), full)
        out_ref[c] = full.astype(BF16)


def turned(v):
    return jnp.concatenate([v[:, 64:], v[:, :64]], axis=1)


def rim_kernel(run_ref, low_ref, high_ref):
    low_ref[:, 0:16] = run_ref[5, :, 32:48]
    low_ref[:, 16:64] = run_ref[6]
    low_ref[:, 64:112] = run_ref[7]
    high_ref[:, 0:48] = run_ref[0]
    high_ref[:, 48:96] = run_ref[1]
    high_ref[:, 96:112] = run_ref[2, :, 0:16]


def zonal_kernel(low_ref, mid_ref, high_ref, toep_ref, zonal):
    lane = lax.broadcasted_iota(jnp.int32, (SLOT, 128), 1)
    first_half = lane < 64
    tile_row = lax.broadcasted_iota(jnp.int32, (16, 128), 0)

    def block(b, c):
        if 0 <= b < BLOCKS:
            return mid_ref[b, c]
        if b < 0:
            return low_ref[c, 16 + SLOT * (b + 2) : 16 + SLOT * (b + 3)]
        return high_ref[c, SLOT * (b - BLOCKS) : SLOT * (b - BLOCKS + 1)]

    def one_pair(c):
        blocks = {b: block(b, c) for b in range(-2, BLOCKS + 2)}
        tails = {b: blocks[b][32:48] if b >= -2 else low_ref[c, 0:16] for b in range(-3, 5)}
        heads = {
            b: blocks[b][0:16] if b < BLOCKS + 2 else high_ref[c, 2 * SLOT : 2 * SLOT + 16]
            for b in range(3, BLOCKS + 3)
        }
        blocks_turned = {b: turned(v) for b, v in blocks.items()}
        tails_turned = {b: turned(v) for b, v in tails.items()}
        heads_turned = {b: turned(v) for b, v in heads.items()}
        for part in range(2):

            def paired(plain, other, b):
                low, high = (plain, other) if part == 0 else (other, plain)
                return jnp.where(first_half[: low[b].shape[0]], low[b], high[b + 4])

            wide = {b: paired(blocks, blocks_turned, b) for b in range(-2, 6)}
            taps = toep_ref[part * 8 + c]
            windows = []
            for b in range(4):
                rim = jnp.where(
                    tile_row >= 8,
                    paired(tails, tails_turned, b - 3),
                    paired(heads, heads_turned, b + 3),
                )
                windows.append(
                    jnp.concatenate([wide[b + k] for k in range(-2, 3)] + [rim], axis=0)
                )
            for b in (0, 2):
                window = jnp.concatenate(windows[b : b + 2], axis=1)
                result = jnp.dot(taps, window, preferred_element_type=F32)
                for k in range(2):
                    first = (b + k) * TALL * GROUP + part * 8 + c
                    zonal[pl.ds(first, TALL, stride=GROUP), :] = result[:, k * 128 : k * 128 + 128]

    for c in range(8):
        one_pair(c)


def conv_kernel(unused_ref, zonal, weight_ref, out_ref, shifted):
    place = lax.broadcasted_iota(jnp.int32, (TALL * GROUP, 128), 1) % 64
    for b in range(4):
        z = zonal[b * TALL * GROUP : (b + 1) * TALL * GROUP, :].astype(BF16)
        zero = jnp.zeros_like(z)
        south = jnp.where(place < 2, zero, jnp.concatenate([z[:, 126:], z[:, :126]], axis=1))
        north = jnp.where(place >= 62, zero, jnp.concatenate([z[:, 2:], z[:, :2]], axis=1))
        for a, v in enumerate((south, z, north)):
            shifted[b, a] = v.reshape(TALL, GROUP, 128)

    weight = weight_ref[...]

    def three_columns(n, carry):
        for half in range(2):
            for i in range(3):
                col = n * 3 + i
                sides = []
                for top in range(2):
                    tiles = [
                        shifted[half + 2 * top, a, col + 4 * b] for b in range(3) for a in range(3)
                    ]
                    sides.append(jnp.concatenate(tiles, axis=0))
                x = jnp.dot(weight, jnp.concatenate(sides, axis=1), preferred_element_type=F32)
                x = 0.5 * x * (1.0 + lax.erf(x * 0.7071067811865476))
                x = x.astype(BF16)
                for top in range(2):
                    out_ref[half * 16 + n, top * 3 + i] = x[:, top * 128 : top * 128 + 128]
        return carry

    lax.fori_loop(0, 15, three_columns, 0)
    for half in range(2):
        for i in range(6):
            out_ref[half * 16 + 15, i] = jnp.zeros((GROUP, 128), BF16)


def mix_kernel(owner_ref, weight_ref, hidden_ref, out_ref):
    first_half = lax.broadcasted_iota(jnp.int32, (GROUP, 128), 1) < 64
    weight = weight_ref[...].reshape(512, 512)
    for i in range(3):
        cols = [hidden_ref[:, top * 3 + i].reshape(512, 128) for top in range(2)]
        y = jnp.dot(weight, jnp.concatenate(cols, axis=1), preferred_element_type=F32)
        y = y.astype(BF16)
        for ch in range(16):
            owner = owner_ref[ch]
            for top in range(2):
                a = y[ch * 32 : ch * 32 + 16, top * 128 : top * 128 + 128]
                b = y[ch * 32 + 16 : ch * 32 + 32, top * 128 : top * 128 + 128]
                out_ref[top, owner, i] = jnp.where(first_half, a, turned(b))
                out_ref[2 + top, owner, i] = jnp.where(first_half, turned(a), b)


def join_kernel(mixed_ref, fields_ref, out_ref):
    shuffle = lat_shuffle(True)
    for m in range(MEMBERS):
        both = jnp.concatenate(
            [mixed_ref[m, s, 0:WIDTH].reshape(WIDTH * GROUP, 128) for s in range(2)], axis=1
        )
        y = jnp.dot(both, shuffle, preferred_element_type=F32).reshape(WIDTH, GROUP, 256)
        for part in range(2):
            rows = slice(part * GROUP, part * GROUP + GROUP)
            total = fields_ref[m, :, rows].astype(F32) + y[:, :, part * 128 : part * 128 + 128]
            out_ref[m, :, rows] = total.astype(BF16)


def kernel_call(body, shape, scratch=(), cost=(0, 0), **specs):
    return pl.pallas_call(
        body,
        **specs,
        out_shape=shape if isinstance(shape, list) else jax.ShapeDtypeStruct(shape, BF16),
        scratch_shapes=list(scratch),
        compiler_params=VMEM,
        cost_estimate=pl.CostEstimate(flops=cost[0], bytes_accessed=cost[1], transcendentals=0),
    )


def from_behind(blocks, axis, step):
    count = lax.axis_size(axis)
    return lax.ppermute(blocks, axis, [(i, (i + step) % count) for i in range(count)])


def block_owners():
    i = jnp.arange(16)
    i = jnp.where(i < 8, i, 8 + (i + 4 * lax.axis_index("core")) % 8)
    zh = (lax.axis_index("zh") + i // 8) % 2
    y = (lax.axis_index("y") - 4 + i) % 8
    return (zh * 8 + y).astype(jnp.int32)


def per_device(fields, zonal_taps, conv_weight, mix_weight):
    core = lax.axis_index("core")
    vmem = pl.BlockSpec(memory_space=pltpu.VMEM)
    loose = pl.BlockSpec(memory_space=pl.ANY)
    by_group = mix_weight.reshape(CHANS, 16, 2, GROUP).transpose(0, 2, 1, 3).reshape(CHANS, 512)
    few = by_group[None]
    few = jnp.concatenate([from_behind(few, "y", 1), few, from_behind(few, "y", -1)], axis=0)
    few = jnp.concatenate(
        [from_behind(few, "y", 3), few, from_behind(few[:2], "y", -3)], axis=0
    )
    half = from_behind(lax.dynamic_slice_in_dim(few, 4 * core, 4, 0), "zh", 1)
    mix_full = jnp.concatenate([few, half, from_behind(half, "core", 1)], axis=0)

    columns = fields.transpose(0, 2, 1, 3)
    units = kernel_call(
        split_kernel,
        (2, 2, 2, 8, SLOT, 128),
        scratch=(pltpu.VMEM((WIDTH * CHANS, 128), F32),),
        cost=(2 * 10**8, 3 * 10**6),
        grid=(MEMBERS,),
        in_specs=[pl.BlockSpec((1, WIDTH, CHANS, 128), lambda m: (m, 0, 0, 0))],
        out_specs=pl.BlockSpec((1, 2, 2, 8, SLOT, 128), lambda m: (m, 0, 0, 0, 0, 0)),
    )(columns)
    run = lax.all_to_all(
        units.reshape(BLOCKS, 8, SLOT, 128), ("zl", "core"), 0, 0, tiled=True
    )
    taps = lax.dynamic_slice_in_dim(zonal_taps, core * GROUP, GROUP, 0).astype(F32)
    taps = jnp.pad(taps, ((0, 0), (0, 256 - taps.shape[1])))
    toeplitz = kernel_call(toeplitz_kernel, (GROUP, TALL, 256), cost=(10**7, 10**6))(taps)
    weight = lax.dynamic_slice_in_dim(conv_weight, core * GROUP, GROUP, 0)
    weight = weight.transpose(0, 3, 2, 1).reshape(GROUP, 9 * GROUP)

    count = lax.axis_size("x")
    east = [(i, (i + 1) % count) for i in range(count)]
    west = [(b, a) for a, b in east]
    rim = jax.ShapeDtypeStruct((8, 112, 128), BF16)
    low, high = kernel_call(rim_kernel, [rim, rim], cost=(0, 10**6))(run)
    low = lax.ppermute(low, "x", east)
    high = lax.ppermute(high, "x", west)

    zonal_shape = [jax.ShapeDtypeStruct((4 * TALL * GROUP, 128), F32)]
    zonal = kernel_call(zonal_kernel, zonal_shape, cost=(10**9, 3 * 10**6))(
        low, run, high, toeplitz
    )[0]
    hidden = kernel_call(
        conv_kernel,
        (32, 6, GROUP, 128),
        scratch=(pltpu.VMEM((4, 3, TALL, GROUP, 128), BF16),),
        cost=(10**9, 3 * 10**6),
        in_specs=[loose, vmem, vmem],
    )(half, zonal, weight)
    gathered = lax.all_to_all(hidden, ("core", "zh", "y"), 0, 0, tiled=True)
    mixed = kernel_call(
        mix_kernel,
        (4, 16, 3, GROUP, 128),
        cost=(4 * 10**8, 2 * 10**6),
        in_specs=[pl.BlockSpec(memory_space=pltpu.SMEM), vmem, vmem],
    )(block_owners(), mix_full, gathered)
    back = lax.all_to_all(mixed.reshape(64, 3, GROUP, 128), ("zl", "zh", "y"), 0, 0, tiled=True)
    updated = kernel_call(join_kernel, columns.shape, cost=(2 * 10**8, 3 * 10**6))(
        back.reshape(MEMBERS, 2, SLOT, GROUP, 128), columns
    )
    return updated.transpose(0, 2, 1, 3)


def solution(mesh):
    names, sizes = zip(*CHIPS)
    chips = Mesh(mesh.devices.reshape(sizes), names)
    lon, ch = ("x", "zl", "core"), ("zh", "y")
    return jax.shard_map(
        per_device,
        mesh=chips,
        in_specs=(P(None, ch, lon, None), P(ch, None), P(ch, None, None, None), P(ch, None)),
        out_specs=P(None, ch, lon, None),
        check_vma=False,
    )
```

```python
import jax
import jax.numpy as jnp
from jax import lax
from jax.experimental import pallas as pl
from jax.experimental.pallas import tpu as pltpu
from jax.sharding import Mesh, PartitionSpec as P

F32, BF16 = jnp.float32, jnp.bfloat16
MEMBERS, CHANS, WIDTH, LAT = 2, 32, 45, 128
SLOT = 48
GROUP = 16
TALL = 56
BLOCKS = 8
VMEM = pltpu.CompilerParams(vmem_limit_bytes=40 * 1024 * 1024)
CHIPS = (("x", 4), ("zl", 4), ("core", 2), ("zh", 2), ("y", 8))


def lat_shuffle(back):
    rows = lax.broadcasted_iota(jnp.int32, (256, 256), 1 if back else 0)
    cols = lax.broadcasted_iota(jnp.int32, (256, 256), 0 if back else 1)
    chan, lane = (cols % 128) // 64, cols % 64
    source = chan * 128 + 4 * (lane // 2) + 2 * (cols // 128) + lane % 2
    return jnp.where(rows == source, 1.0, 0.0).astype(BF16)


def split_kernel(fields_ref, out_ref, wide):
    shuffle = lat_shuffle(False)
    wide[...] = fields_ref[...].astype(F32).reshape(MEMBERS, WIDTH * CHANS, 128)
    for m in range(MEMBERS):
        for g in range(2):
            for c in range(8):
                sides = [
                    wide[m, pl.ds(g * GROUP + part * 8 + c, WIDTH, stride=CHANS), :].astype(BF16)
                    for part in range(2)
                ]
                both = jnp.concatenate(sides, axis=1)
                moved = jnp.dot(both, shuffle, preferred_element_type=F32).astype(BF16)
                for s in range(2):
                    out_ref[m, s, g, c, 32:48] = jnp.zeros((16, 128), BF16)
                    out_ref[m, s, g, c, 0:WIDTH] = moved[:, s * 128 : s * 128 + 128]


def toeplitz_kernel(taps_ref, out_ref):
    lane = lax.broadcasted_iota(jnp.int32, (TALL, 256), 1)
    for c in range(GROUP):
        row = jnp.broadcast_to(taps_ref[c : c + 1, :], (TALL, 256))
        base = pltpu.roll(row, 0, 1, stride=1, stride_axis=0)
        full = pltpu.roll(base, 252, 1)
        for k in range(1, 5):
            full = jnp.where(lane >= SLOT * k, pltpu.roll(base, (3 * k - 4) % 256, 1), full)
        full = jnp.where(lane >= 240, pltpu.roll(base, 11, 1), full)
        full = jnp.where(lane >= 248, pltpu.roll(base, 249, 1), full)
        out_ref[c] = full.astype(BF16)


def turned(v):
    return jnp.concatenate([v[:, 64:], v[:, :64]], axis=1)


def rim_kernel(run_ref, unused_ref, low_ref, high_ref):
    low_ref[:, 0:16] = run_ref[5, :, 32:48]
    low_ref[:, 16:64] = run_ref[6]
    low_ref[:, 64:112] = run_ref[7]
    high_ref[:, 0:48] = run_ref[0]
    high_ref[:, 48:96] = run_ref[1]
    high_ref[:, 96:112] = run_ref[2, :, 0:16]


def zonal_kernel(low_ref, mid_ref, high_ref, toep_ref, zonal):
    lane = lax.broadcasted_iota(jnp.int32, (SLOT, 128), 1)
    first_half = lane < 64
    tile_row = lax.broadcasted_iota(jnp.int32, (16, 128), 0)

    def block(b, c):
        if 0 <= b < BLOCKS:
            return mid_ref[b, c]
        if b < 0:
            return low_ref[c, 16 + SLOT * (b + 2) : 16 + SLOT * (b + 3)]
        return high_ref[c, SLOT * (b - BLOCKS) : SLOT * (b - BLOCKS + 1)]

    def one_pair(c):
        blocks = {b: block(b, c) for b in range(-2, BLOCKS + 2)}
        tails = {b: blocks[b][32:48] if b >= -2 else low_ref[c, 0:16] for b in range(-3, 5)}
        heads = {
            b: blocks[b][0:16] if b < BLOCKS + 2 else high_ref[c, 2 * SLOT : 2 * SLOT + 16]
            for b in range(3, BLOCKS + 3)
        }
        blocks_turned = {b: turned(v) for b, v in blocks.items()}
        tails_turned = {b: turned(v) for b, v in tails.items()}
        heads_turned = {b: turned(v) for b, v in heads.items()}
        for part in range(2):

            def paired(plain, other, b):
                low, high = (plain, other) if part == 0 else (other, plain)
                return jnp.where(first_half[: low[b].shape[0]], low[b], high[b + 4])

            wide = {b: paired(blocks, blocks_turned, b) for b in range(-2, 6)}
            taps = toep_ref[part * 8 + c]
            windows = []
            for b in range(4):
                rim = jnp.where(
                    tile_row >= 8,
                    paired(tails, tails_turned, b - 3),
                    paired(heads, heads_turned, b + 3),
                )
                windows.append(
                    jnp.concatenate([wide[b + k] for k in range(-2, 3)] + [rim], axis=0)
                )
            for b in (0, 2):
                window = jnp.concatenate(windows[b : b + 2], axis=1)
                result = jnp.dot(taps, window, preferred_element_type=F32)
                for k in range(2):
                    first = (b + k) * TALL * GROUP + part * 8 + c
                    zonal[pl.ds(first, TALL, stride=GROUP), :] = result[:, k * 128 : k * 128 + 128]

    for c in range(8):
        one_pair(c)


def conv_kernel(unused_ref, zonal, weight_ref, out_ref, shifted):
    place = lax.broadcasted_iota(jnp.int32, (TALL * GROUP, 128), 1) % 64
    for b in range(4):
        z = zonal[b * TALL * GROUP : (b + 1) * TALL * GROUP, :].astype(BF16)
        zero = jnp.zeros_like(z)
        south = jnp.where(place < 2, zero, jnp.concatenate([z[:, 126:], z[:, :126]], axis=1))
        north = jnp.where(place >= 62, zero, jnp.concatenate([z[:, 2:], z[:, :2]], axis=1))
        for a, v in enumerate((south, z, north)):
            shifted[b, a] = v.reshape(TALL, GROUP, 128)

    weight = weight_ref[...]

    def three_columns(n, carry):
        for half in range(2):
            for i in range(3):
                col = n * 3 + i
                sides = []
                for top in range(2):
                    tiles = [
                        shifted[half + 2 * top, a, col + 4 * b] for b in range(3) for a in range(3)
                    ]
                    sides.append(jnp.concatenate(tiles, axis=0))
                x = jnp.dot(weight, jnp.concatenate(sides, axis=1), preferred_element_type=F32)
                x = 0.5 * x * (1.0 + lax.erf(x * 0.7071067811865476))
                x = x.astype(BF16)
                for top in range(2):
                    out_ref[half * 16 + n, top * 3 + i] = x[:, top * 128 : top * 128 + 128]
        return carry

    lax.fori_loop(0, 15, three_columns, 0)
    for half in range(2):
        for i in range(6):
            out_ref[half * 16 + 15, i] = jnp.zeros((GROUP, 128), BF16)


def mix_kernel(owner_ref, weight_ref, hidden_ref, out_ref):
    first_half = lax.broadcasted_iota(jnp.int32, (GROUP, 128), 1) < 64
    weight = weight_ref[...].reshape(512, 512)
    for i in range(3):
        cols = [hidden_ref[:, top * 3 + i].reshape(512, 128) for top in range(2)]
        y = jnp.dot(weight, jnp.concatenate(cols, axis=1), preferred_element_type=F32)
        y = y.astype(BF16)
        for ch in range(16):
            owner = owner_ref[ch]
            for top in range(2):
                a = y[ch * 32 : ch * 32 + 16, top * 128 : top * 128 + 128]
                b = y[ch * 32 + 16 : ch * 32 + 32, top * 128 : top * 128 + 128]
                out_ref[top, owner, i] = jnp.where(first_half, a, turned(b))
                out_ref[2 + top, owner, i] = jnp.where(first_half, turned(a), b)


def join_kernel(mixed_ref, fields_ref, out_ref):
    shuffle = lat_shuffle(True)
    for m in range(MEMBERS):
        both = jnp.concatenate(
            [mixed_ref[m, s, 0:WIDTH].reshape(WIDTH * GROUP, 128) for s in range(2)], axis=1
        )
        y = jnp.dot(both, shuffle, preferred_element_type=F32).reshape(WIDTH, GROUP, 256)
        for part in range(2):
            rows = slice(part * GROUP, part * GROUP + GROUP)
            total = fields_ref[m, :, rows].astype(F32) + y[:, :, part * 128 : part * 128 + 128]
            out_ref[m, :, rows] = total.astype(BF16)


def kernel_call(body, shape, scratch=(), cost=(0, 0), **specs):
    return pl.pallas_call(
        body,
        **specs,
        out_shape=shape if isinstance(shape, list) else jax.ShapeDtypeStruct(shape, BF16),
        scratch_shapes=list(scratch),
        compiler_params=VMEM,
        cost_estimate=pl.CostEstimate(flops=cost[0], bytes_accessed=cost[1], transcendentals=0),
    )


def from_behind(blocks, axis, step):
    count = lax.axis_size(axis)
    return lax.ppermute(blocks, axis, [(i, (i + step) % count) for i in range(count)])


def block_owners():
    i = jnp.arange(16)
    i = jnp.where(i < 8, i, 8 + (i + 4 * lax.axis_index("core")) % 8)
    zh = (lax.axis_index("zh") + i // 8) % 2
    y = (lax.axis_index("y") - 4 + i) % 8
    return (zh * 8 + y).astype(jnp.int32)


def per_device(fields, zonal_taps, conv_weight, mix_weight):
    core = lax.axis_index("core")
    vmem = pl.BlockSpec(memory_space=pltpu.VMEM)
    loose = pl.BlockSpec(memory_space=pl.ANY)
    by_group = mix_weight.reshape(CHANS, 16, 2, GROUP).transpose(0, 2, 1, 3).reshape(CHANS, 512)
    few = by_group[None]
    few = jnp.concatenate([from_behind(few, "y", 1), few, from_behind(few, "y", -1)], axis=0)
    few = jnp.concatenate(
        [from_behind(few, "y", 3), few, from_behind(few[:2], "y", -3)], axis=0
    )
    half = from_behind(lax.dynamic_slice_in_dim(few, 4 * core, 4, 0), "zh", 1)
    mix_full = jnp.concatenate([few, half, from_behind(half, "core", 1)], axis=0)

    columns = fields.transpose(0, 2, 1, 3)
    units = kernel_call(
        split_kernel,
        (2, 2, 2, 8, SLOT, 128),
        scratch=(pltpu.VMEM((MEMBERS, WIDTH * CHANS, 128), F32),),
        cost=(2 * 10**8, 3 * 10**6),
    )(columns)
    run = lax.all_to_all(
        units.reshape(BLOCKS, 8, SLOT, 128), ("zl", "core"), 0, 0, tiled=True
    )
    taps = lax.dynamic_slice_in_dim(zonal_taps, core * GROUP, GROUP, 0).astype(F32)
    taps = jnp.pad(taps, ((0, 0), (0, 256 - taps.shape[1])))
    toeplitz = kernel_call(toeplitz_kernel, (GROUP, TALL, 256), cost=(10**7, 10**6))(taps)
    weight = lax.dynamic_slice_in_dim(conv_weight, core * GROUP, GROUP, 0)
    weight = weight.transpose(0, 3, 2, 1).reshape(GROUP, 9 * GROUP)

    count = lax.axis_size("x")
    east = [(i, (i + 1) % count) for i in range(count)]
    west = [(b, a) for a, b in east]
    rim = jax.ShapeDtypeStruct((8, 112, 128), BF16)
    low, high = kernel_call(rim_kernel, [rim, rim], in_specs=[vmem, loose], cost=(0, 10**6))(run, toeplitz)
    low = lax.ppermute(low, "x", east)
    high = lax.ppermute(high, "x", west)

    zonal_shape = [jax.ShapeDtypeStruct((4 * TALL * GROUP, 128), F32)]
    zonal = kernel_call(zonal_kernel, zonal_shape, cost=(10**9, 3 * 10**6))(
        low, run, high, toeplitz
    )[0]
    hidden = kernel_call(
        conv_kernel,
        (32, 6, GROUP, 128),
        scratch=(pltpu.VMEM((4, 3, TALL, GROUP, 128), BF16),),
        cost=(10**9, 3 * 10**6),
        in_specs=[loose, vmem, vmem],
    )(half, zonal, weight)
    gathered = lax.all_to_all(hidden, ("core", "zh", "y"), 0, 0, tiled=True)
    mixed = kernel_call(
        mix_kernel,
        (4, 16, 3, GROUP, 128),
        cost=(4 * 10**8, 2 * 10**6),
        in_specs=[pl.BlockSpec(memory_space=pltpu.SMEM), vmem, vmem],
    )(block_owners(), mix_full, gathered)
    back = lax.all_to_all(mixed.reshape(64, 3, GROUP, 128), ("zl", "zh", "y"), 0, 0, tiled=True)
    updated = kernel_call(join_kernel, columns.shape, cost=(2 * 10**8, 3 * 10**6))(
        back.reshape(MEMBERS, 2, SLOT, GROUP, 128), columns
    )
    return updated.transpose(0, 2, 1, 3)


def solution(mesh):
    names, sizes = zip(*CHIPS)
    chips = Mesh(mesh.devices.reshape(sizes), names)
    lon, ch = ("x", "zl", "core"), ("zh", "y")
    return jax.shard_map(
        per_device,
        mesh=chips,
        in_specs=(P(None, ch, lon, None), P(ch, None), P(ch, None, None, None), P(ch, None)),
        out_specs=P(None, ch, lon, None),
        check_vma=False,
    )
```
